32 devices in a mesh: dp: 8 (over z, y), tensor: 4 (over x, core).
Axes of the slice: x: 2, y: 2, z: 4, core: 2. Of those that a mesh axis runs over, the one named last changes fastest.
Arguments:
- tokens: bfloat16 [8192, 1024], P('dp'), may hold values from -6 to 6
- segment_ids: int32 [8, 1024], P('dp'), may hold values from 0 to 3, never falling along the last dimension, each value on 1 to 512 neighbouring positions
- cotangent: bfloat16 [8192, 1024], P('dp'), may hold values from -6 to 6
- attn_gain: bfloat16 [1024], P('dp'), may hold values from 0.099609375 to 1.8984375
- query_gain: bfloat16 [64], P('dp'), may hold values from 0.099609375 to 1.8984375
- key_gain: bfloat16 [64], P('dp'), may hold values from 0.099609375 to 1.8984375
- w_query: bfloat16 [1024, 1024], P('dp', 'tensor'), may hold values from -0.1875 to 0.1875
- w_key: bfloat16 [1024, 512], P('dp', 'tensor'), may hold values from -0.1875 to 0.1875
- w_value: bfloat16 [1024, 512], P('dp', 'tensor'), may hold values from -0.1875 to 0.1875
- w_out: bfloat16 [1024, 1024], P('tensor', 'dp'), may hold values from -0.75 to 0.75
- ffn_gain: bfloat16 [1024], P('dp'), may hold values from 0.099609375 to 1.8984375
- w_gate: bfloat16 [1024, 4608], P('dp', 'tensor'), may hold values from -0.1875 to 0.1875
- w_up: bfloat16 [1024, 4608], P('dp', 'tensor'), may hold values from -0.1875 to 0.1875
- w_down: bfloat16 [4608, 1024], P('tensor', 'dp'), may hold values from -0.09375 to 0.09375
Outputs:
- output: bfloat16 [8192, 1024], P('dp')
- d_tokens: float32 [8192, 1024], P('dp')
- d_attn_gain: float32 [1024], P('dp')
- d_query_gain: float32 [64], P('dp')
- d_key_gain: float32 [64], P('dp')
- d_w_query: float32 [1024, 1024], P('dp', 'tensor')
- d_w_key: float32 [1024, 512], P('dp', 'tensor')
- d_w_value: float32 [1024, 512], P('dp', 'tensor')
- d_w_out: float32 [1024, 1024], P('tensor', 'dp')
- d_ffn_gain: float32 [1024], P('dp')
- d_w_gate: float32 [1024, 4608], P('dp', 'tensor')
- d_w_up: float32 [1024, 4608], P('dp', 'tensor')
- d_w_down: float32 [4608, 1024], P('tensor', 'dp')
The draws below stay inside these ranges and needn't reach their ends.
Inputs may be any that keep to these rules, and one draw needn't show every extreme that they name: `segment_ids`: in each row, sequence numbers never fall and run through 0 to 3; each sequence has 1 to 512 slots and one sequence of each row has exactly 512.
All inputs are finite; a program needn't handle non-finite values.
Results may differ from the reference program's by a relative error of at most 0.012.
The reference program's roundings to bfloat16 on the way count: a program that leaves them out, or rounds other values in their place, can miss the bound.
Values may be sent and summed in bfloat16 or wider, within the bound.
A program may use at most 128 MiB of HBM per device.

```python
import math
import jax
import jax.numpy as jnp
import numpy as np
from jax import lax

D = 1024
QH = 16
KVH = 8
HD = 64
FF = 4608
TOK_DEV = 1024
MAXLEN = 512
SEQS = 4
QW = 1024
KW = 512
GROUP = 2
TOKENS = 8192
N_DP = 8


def level_of(own_key, extent, split, least, largest):
    level = 1.0
    for position, blocks in split:
        steps = jax.random.uniform(jax.random.fold_in(jax.random.fold_in(own_key, 6), position), (blocks,), jnp.float32, least / len(split), largest / len(split))
        level = level * jnp.repeat(jnp.exp(steps), extent[position] // blocks).reshape((-1,) + (1,) * (len(extent) - 1 - position))
    return level


def profile(number_of, total, reach, lean):
    portions = [(1 << 20) // math.isqrt(rank ** lean) + 1 for rank in range(2, number_of + 1)]
    spare, holding = total - reach - (number_of - 1), [1] * (number_of - 1)
    while spare > 0:
        free = [i for i in range(number_of - 1) if holding[i] < reach]
        whole, left = sum([portions[i] for i in free]), spare
        for i in free:
            more = min(reach - holding[i], max(1, left * portions[i] // whole), spare)
            holding[i] = holding[i] + more
            spare = spare - more
    return np.array([reach] + holding)


def uneven(own_key, amount, total, most, skew):
    if amount == 2:
        one = jax.random.randint(own_key, (), max(1, total - most), min(most, total - 1) + 1)
        return jnp.stack([one, total - one])
    sizes = jnp.asarray(profile(amount, total, most, skew), jnp.int32)
    pairs = (amount - 1) // 2
    giver, receiver = sizes[1:1 + 2 * pairs:2], sizes[2:2 + 2 * pairs:2]
    margin = jnp.minimum(giver - 1, most - receiver)
    moved = jax.random.randint(jax.random.fold_in(own_key, 1), (pairs,), 0, 1 << 20) % (margin + 1)
    sizes = sizes.at[1:1 + 2 * pairs:2].set(giver - moved).at[2:2 + 2 * pairs:2].set(receiver + moved)
    return sizes[jax.random.permutation(jax.random.fold_in(own_key, 2), amount)]


def bell_draw(key, shape, deviation, limit, shards=(), held_as=jnp.bfloat16):
    loudness = level_of(key, shape, shards, -0.22, 0.18) if shards else 1.0
    entries = jax.random.normal(key, shape, jnp.float32) * deviation * loudness
    return jnp.minimum(jnp.maximum(entries, -limit), limit).astype(held_as)


def setup_inputs(seed: int = 0) -> dict:
    keys = jax.random.split(jax.random.key(seed), 15)
    return {
        "tokens": bell_draw(keys[0], (TOKENS, D), 1.0, 6.0, ((0, 8),)),
        "segment_ids": jax.vmap(lambda own: jnp.searchsorted(jnp.cumsum(uneven(own, SEQS, TOK_DEV, MAXLEN, 2)), jnp.arange(TOK_DEV), side="right"))(jax.random.split(keys[1], N_DP)).reshape((N_DP, TOK_DEV)).astype(jnp.int32),
        "cotangent": bell_draw(keys[2], (TOKENS, D), 1.0, 6.0, ((0, 8),)),
        "attn_gain": jnp.clip(1.0 + 0.18 * jax.random.normal(keys[3], (D,), jnp.float32), 0.099609375, 1.8984375).astype(jnp.bfloat16),
        "query_gain": jnp.clip(1.0 + 0.18 * jax.random.normal(keys[4], (HD,), jnp.float32), 0.099609375, 1.8984375).astype(jnp.bfloat16),
        "key_gain": jnp.clip(1.0 + 0.18 * jax.random.normal(keys[5], (HD,), jnp.float32), 0.099609375, 1.8984375).astype(jnp.bfloat16),
        "w_query": bell_draw(keys[6], (D, QW), D ** -0.5, 0.1875, ((0, 8), (1, 4))),
        "w_key": bell_draw(keys[7], (D, KW), D ** -0.5, 0.1875, ((0, 8), (1, 4))),
        "w_value": bell_draw(keys[8], (D, KW), D ** -0.5, 0.1875, ((0, 8), (1, 4))),
        "w_out": bell_draw(keys[9], (QW, D), (QW // 16) ** -0.5, 0.75, ((0, 4), (1, 8))),
        "ffn_gain": jnp.clip(1.0 + 0.18 * jax.random.normal(keys[10], (D,), jnp.float32), 0.099609375, 1.8984375).astype(jnp.bfloat16),
        "w_gate": bell_draw(keys[11], (D, FF), D ** -0.5, 0.1875, ((0, 8), (1, 4))),
        "w_up": bell_draw(keys[12], (D, FF), D ** -0.5, 0.1875, ((0, 8), (1, 4))),
        "w_down": bell_draw(keys[13], (FF, D), FF ** -0.5, 0.09375, ((0, 4), (1, 8))),
    }


EPS = 1e-05
THETA = 1000000.0
SCALE = 0.125

@jax.custom_vjp
def low(v):
    return lax.optimization_barrier(v.astype(jnp.bfloat16)).astype(jnp.float32)

@jax.custom_vjp
def low_back(v):
    return v

def low_keep(v):
    return (low(v), None)

def low_pass(kept, grad):
    return (grad,)

def back_keep(v):
    return (v, None)

def back_low(kept, grad):
    return (low(grad),)
low.defvjp(low_keep, low_pass)
low_back.defvjp(back_keep, back_low)

def positions(segs):
    count = segs.shape[0]
    index = jnp.arange(count, dtype=jnp.int32)
    starts = jnp.concatenate([jnp.ones((1,), dtype=bool), segs[1:] != segs[:-1]])
    first = lax.cummax(jnp.where(starts, index, jnp.zeros_like(index)), axis=0)
    return index - first

def rotary_tables(pos, width):
    half = width // 2
    freq = THETA ** (-(jnp.arange(half, dtype=jnp.float32) * 2.0) / width)
    angle = pos.astype(jnp.float32)[:, None] * freq[None, :]
    return (jnp.cos(angle), jnp.sin(angle))

def rotate(values, cosine, sine):
    half = values.shape[-1] // 2
    first, second = (values[..., :half], values[..., half:])
    cos_b = cosine[:, None, :]
    sin_b = sine[:, None, :]
    return jnp.concatenate([first * cos_b - second * sin_b, second * cos_b + first * sin_b], axis=-1)

def row_norm(values, gain):
    return values * lax.rsqrt(lax.optimization_barrier(jnp.mean(values * values, axis=-1, keepdims=True)) + EPS) * gain

def matmul(left, right):
    return jnp.dot(left, right, precision=lax.Precision.HIGHEST, preferred_element_type=jnp.float32)

def forward(inputs, segs, gain_one, gain_query, gain_key, w_query, w_key, w_value, w_out, gain_two, w_gate, w_up, w_down):
    count = inputs.shape[0]
    pos = positions(segs)
    cosine, sine = rotary_tables(pos, HD)
    first_in = low(row_norm(inputs, gain_one))
    query_raw = low_back(matmul(first_in, w_query)).reshape(count, QH, HD)
    key_raw = low_back(matmul(first_in, w_key)).reshape(count, KVH, HD)
    value_low = low(low_back(matmul(first_in, w_value))).reshape(count, KVH, HD)
    query_low = low(rotate(row_norm(query_raw, gain_query), cosine, sine)).reshape(count, KVH, GROUP, HD)
    key_low = low(rotate(row_norm(key_raw, gain_key), cosine, sine))
    scores = low_back(jnp.einsum('qkgd,jkd->kgqj', query_low, key_low, precision=lax.Precision.HIGHEST) * SCALE)
    index = jnp.arange(count, dtype=jnp.int32)
    allowed = (segs[None, :] == segs[:, None]) & (index[None, :] <= index[:, None])
    scores = jnp.where(allowed, scores, -1e+30)
    peak = lax.optimization_barrier(jnp.max(scores, axis=-1, keepdims=True))
    expo = jnp.exp(scores - peak)
    probs = expo / lax.optimization_barrier(jnp.sum(expo, axis=-1, keepdims=True))
    mixed = jnp.einsum('kgqj,jkd->qkgd', low(probs), value_low, precision=lax.Precision.HIGHEST)
    attended = low(low_back(mixed)).reshape(count, QW)
    hidden_in = inputs + low_back(matmul(attended, w_out))
    second_in = low(row_norm(hidden_in, gain_two))
    gate_val = low_back(matmul(second_in, w_gate))
    up_val = low_back(matmul(second_in, w_up))
    inner = low(gate_val * jax.nn.sigmoid(gate_val) * up_val)
    return hidden_in + low_back(matmul(inner, w_down))

def reference(tokens, segment_ids, cotangent, attn_gain, query_gain, key_gain, w_query, w_key, w_value, w_out, ffn_gain, w_gate, w_up, w_down):
    params = tuple((item.astype(jnp.float32) for item in (attn_gain, query_gain, key_gain, w_query, w_key, w_value, w_out, ffn_gain, w_gate, w_up, w_down)))
    inputs = tokens.astype(jnp.float32).reshape(N_DP, TOK_DEV, D)
    cots = cotangent.astype(jnp.float32).reshape(N_DP, TOK_DEV, D)

    def one_group(carry, item):
        group_in, segs, group_cot = item

        def local(values, *weights):
            return forward(values, segs, *weights)
        result, pull = jax.vjp(local, group_in, *params)
        grads = pull(group_cot)
        carry = tuple((left + right for left, right in zip(carry, grads[1:])))
        return (carry, (result.astype(jnp.bfloat16), grads[0]))
    start = tuple((jnp.zeros_like(item) for item in params))
    totals, (outputs, d_inputs) = lax.scan(one_group, start, (inputs, segment_ids, cots))
    return (outputs.reshape(TOKENS, D), d_inputs.reshape(TOKENS, D), totals[0], totals[1], totals[2], totals[3], totals[4], totals[5], totals[6], totals[7], totals[8], totals[9], totals[10])
```

```python
import functools

import jax
import jax.numpy as jnp
from jax import lax
from jax.experimental import pallas as pl
from jax.experimental.pallas import tpu as pltpu
from jax.sharding import PartitionSpec as P

EPS = 1e-05
THETA = 1000000.0
SCALE = 0.125


def positions(segs):
    count = segs.shape[0]
    index = jnp.arange(count, dtype=jnp.int32)
    starts = jnp.concatenate([jnp.ones((1,), dtype=bool), segs[1:] != segs[:-1]])
    first = lax.cummax(jnp.where(starts, index, jnp.zeros_like(index)), axis=0)
    return index - first


def rotary_tables(pos, width):
    half = width // 2
    freq = THETA ** (-(jnp.arange(half, dtype=jnp.float32) * 2.0) / width)
    angle = pos.astype(jnp.float32)[:, None] * freq[None, :]
    return (jnp.cos(angle), jnp.sin(angle))


def rotate(values, cosine, sine):
    half = values.shape[-1] // 2
    first, second = (values[..., :half], values[..., half:])
    cos_b = cosine[:, None, :]
    sin_b = sine[:, None, :]
    return jnp.concatenate(
        [first * cos_b - second * sin_b, second * cos_b + first * sin_b], axis=-1
    )


def unrotate(grads, cosine, sine):
    half = grads.shape[-1] // 2
    first, second = (grads[..., :half], grads[..., half:])
    cos_b = cosine[:, None, :]
    sin_b = sine[:, None, :]
    return jnp.concatenate(
        [first * cos_b + second * sin_b, second * cos_b - first * sin_b], axis=-1
    )


def norm_forward(values, gain):
    inverse = lax.rsqrt(jnp.mean(values * values, axis=-1, keepdims=True) + EPS)
    return (values * inverse * gain, inverse)


def norm_backward(grad_normed, values, inverse, gain):
    scaled = grad_normed * gain
    d_values = inverse * scaled - values * inverse * inverse * inverse * jnp.mean(
        scaled * values, axis=-1, keepdims=True
    )
    flat = (grad_normed * values * inverse).reshape(-1, values.shape[-1])
    return (d_values, jnp.sum(flat, axis=0))


def contract_rows(left, right):
    return lax.dot_general(
        left, right, (((0,), (0,)), ((), ())), preferred_element_type=jnp.float32
    )


def contract_cols(left, right):
    return lax.dot_general(
        left, right, (((1,), (1,)), ((), ())), preferred_element_type=jnp.float32
    )


def block_scores(query_low, key_pad, seg_pad, segs, block, span):
    rows = query_low[block * span : (block + 1) * span]
    keys = key_pad[block * span : block * span + 2 * span]
    scores = jnp.einsum("qkgd,jkd->kgqj", rows, keys, preferred_element_type=jnp.float32) * SCALE
    row_index = block * span + jnp.arange(span, dtype=jnp.int32)
    key_index = block * span - span + jnp.arange(2 * span, dtype=jnp.int32)
    same = (
        seg_pad[block * span : block * span + 2 * span][None, :]
        == segs[block * span : (block + 1) * span][:, None]
    )
    allowed = same & (key_index[None, :] <= row_index[:, None])
    return (jnp.where(allowed, scores, -1e30), rows, keys)


MESH = pl.DeviceIdType.MESH
VMEM_BYTES = 48 * 1024 * 1024
LANES = 128


def whole_vmem():
    return pl.BlockSpec(memory_space=pltpu.VMEM)


def ring_place(index, count):
    odd = lax.rem(index, 2)
    half = lax.div(index, 2)
    return (1 - odd) * half + odd * (count - 1 - half)


def ring_index(place, count):
    second = lax.div(place, count // 2)
    return (1 - second) * 2 * place + second * (2 * (count - 1 - place) + 1)


def ring_parts(width):
    tiles = width // LANES
    cuts = [0, (tiles + 3) // 4, (tiles + 1) // 2, (3 * tiles + 3) // 4, tiles]
    return [
        (cuts[i] * LANES, (cuts[i + 1] - cuts[i]) * LANES, 1 if i < 2 else -1) for i in (0, 2, 1, 3)
    ]


def greet(axis, neighbours):
    barrier = pltpu.get_barrier_semaphore()
    for neighbour in neighbours:
        pl.semaphore_signal(barrier, inc=1, device_id={axis: neighbour}, device_id_type=MESH)
    pl.semaphore_wait(barrier, len(neighbours))


def gather_kernel(count, x_ref, o_ref, own_sem, send_sem, recv_sem):
    me = ring_place(lax.axis_index("dp"), count)
    rows = x_ref.shape[0]
    parts = ring_parts(x_ref.shape[1])
    towards = {way: ring_index(lax.rem(me + way + count, count), count) for way in (1, -1)}
    greet("dp", (towards[1], towards[-1]))

    def block(place, part):
        start, width, _ = parts[part]
        first = pl.multiple_of(ring_index(lax.rem(place + 2 * count, count), count) * rows, rows)
        return o_ref.at[pl.ds(first, rows), pl.ds(start, width)]

    def copy(step, part, source, place):
        start, width, way = parts[part]
        return pltpu.make_async_remote_copy(
            src_ref=source,
            dst_ref=block(place, part),
            send_sem=send_sem.at[part, step],
            recv_sem=recv_sem.at[part, step],
            device_id={"dp": towards[way]},
            device_id_type=MESH,
        )

    def outgoing(step, part):
        place = me - parts[part][2] * step
        return copy(step, part, block(place, part), place)

    def incoming(step, part):
        place = me - parts[part][2] * (step + 1)
        return copy(step, part, block(place, part), place)

    for part, (start, width, _) in enumerate(parts):
        copy(0, part, x_ref.at[:, pl.ds(start, width)], me).start()
    first = pl.multiple_of(ring_index(me, count) * rows, rows)
    own = pltpu.make_async_copy(x_ref, o_ref.at[pl.ds(first, rows)], own_sem)
    own.start()

    def forward(step, carry):
        for part in range(len(parts)):
            incoming(step - 1, part).wait_recv()
            outgoing(step, part).start()
        return carry

    lax.fori_loop(1, count - 1, forward, 0)

    def settle(step, carry):
        for part in range(len(parts)):
            outgoing(step, part).wait_send()
        return carry

    for part in range(len(parts)):
        incoming(count - 2, part).wait_recv()
    lax.fori_loop(0, count - 1, settle, 0)
    own.wait()


def ring_gather(shard, count, ident):
    rows, width = shard.shape
    return pl.pallas_call(
        functools.partial(gather_kernel, count),
        out_shape=jax.ShapeDtypeStruct((rows * count, width), shard.dtype),
        in_specs=[pl.BlockSpec(memory_space=pl.ANY)],
        out_specs=pl.BlockSpec(memory_space=pl.ANY),
        scratch_shapes=[
            pltpu.SemaphoreType.DMA,
            pltpu.SemaphoreType.DMA((4, count - 1)),
            pltpu.SemaphoreType.DMA((4, count - 1)),
        ],
        compiler_params=pltpu.CompilerParams(
            collective_id=ident, has_side_effects=True, vmem_limit_bytes=VMEM_BYTES
        ),
    )(shard)


def scatter_kernel(count, g_ref, o_ref, held, send_sem, recv_sem):
    me = ring_place(lax.axis_index("dp"), count)
    rows = o_ref.shape[0]
    parts = ring_parts(o_ref.shape[1])
    towards = {way: ring_index(lax.rem(me + way + count, count), count) for way in (1, -1)}
    greet("dp", (towards[1], towards[-1]))

    def term(place, part):
        start, width, _ = parts[part]
        first = pl.multiple_of(ring_index(lax.rem(place + 2 * count, count), count) * rows, rows)
        return g_ref.at[pl.ds(first, rows), pl.ds(start, width)]

    def slot(step, part):
        start, width, _ = parts[part]
        return held.at[step, :, pl.ds(start, width)]

    def copy(step, part, source):
        return pltpu.make_async_remote_copy(
            src_ref=source,
            dst_ref=slot(step, part),
            send_sem=send_sem.at[part, step],
            recv_sem=recv_sem.at[part, step],
            device_id={"dp": towards[parts[part][2]]},
            device_id_type=MESH,
        )

    for part, (_, _, way) in enumerate(parts):
        copy(0, part, term(me - way, part)).start()

    def forward(step, carry):
        for part, (_, _, way) in enumerate(parts):
            copy(step - 1, part, slot(step - 1, part)).wait_recv()
            mine = term(me - way * (step + 1), part)
            both = slot(step - 1, part)
            both[...] = (both[...].astype(jnp.float32) + mine[...].astype(jnp.float32)).astype(
                jnp.bfloat16
            )
            copy(step, part, both).start()
        return carry

    lax.fori_loop(1, count - 1, forward, 0)
    for part, (start, width, _) in enumerate(parts):
        copy(count - 2, part, slot(count - 2, part)).wait_recv()
        o_ref[:, pl.ds(start, width)] = slot(count - 2, part)[...].astype(jnp.float32) + term(
            me, part
        )[...].astype(jnp.float32)

    def settle(step, carry):
        for part in range(len(parts)):
            copy(step, part, slot(step, part)).wait_send()
        return carry

    lax.fori_loop(0, count - 1, settle, 0)


def ring_scatter(terms, count, ident):
    total, width = terms.shape
    rows = total // count
    return pl.pallas_call(
        functools.partial(scatter_kernel, count),
        out_shape=jax.ShapeDtypeStruct((rows, width), jnp.float32),
        in_specs=[whole_vmem()],
        out_specs=whole_vmem(),
        scratch_shapes=[
            pltpu.VMEM((count - 1, rows, width), jnp.bfloat16),
            pltpu.SemaphoreType.DMA((4, count - 1)),
            pltpu.SemaphoreType.DMA((4, count - 1)),
        ],
        compiler_params=pltpu.CompilerParams(
            collective_id=ident, has_side_effects=True, vmem_limit_bytes=VMEM_BYTES
        ),
    )(terms)


class Square:
    def __init__(self, rows):
        self.me = lax.axis_index("tensor")
        self.core = lax.rem(self.me, 2)
        self.chip = lax.div(self.me, 2)
        self.beside = self.me + 1 - 2 * self.core
        self.across = lax.rem(self.me + 2, 4)
        self.corner = lax.rem(self.beside + 2, 4)
        self.rows = rows // 4

    def quarter(self, index):
        return pl.ds(pl.multiple_of(index * self.rows, self.rows), self.rows)

    def greet(self, everyone=False):
        partners = (self.beside, self.across)
        greet("tensor", partners + ((self.corner,) if everyone else ()))

    def copy(self, source, target, sems, index, other):
        return pltpu.make_async_remote_copy(
            src_ref=source,
            dst_ref=target,
            send_sem=sems.at[0, index],
            recv_sem=sems.at[1, index],
            device_id={"tensor": other},
            device_id_type=MESH,
        )

    def reduce_start(self, part, held, sems):
        first = self.copy(
            part.at[self.quarter(self.corner)], held.at[0], sems, 0, self.beside
        )
        first.start()
        second = self.copy(
            part.at[self.quarter(self.beside)], held.at[1], sems, 1, self.beside
        )
        second.start()
        return (first, second)

    def reduce_cross(self, part, held, sems, copies):
        copies[0].wait_recv()
        held[3] = (
            part[self.quarter(self.across), :].astype(jnp.float32) + held[0].astype(jnp.float32)
        ).astype(jnp.bfloat16)
        third = self.copy(held.at[3], held.at[2], sems, 2, self.across)
        third.start()
        return copies + (third,)

    def reduce_end(self, part, held, copies):
        copies[1].wait_recv()
        near = part[self.quarter(self.me), :].astype(jnp.float32) + held[1].astype(jnp.float32)
        copies[2].wait_recv()
        total = near + held[2].astype(jnp.float32)
        for copy in copies:
            copy.wait_send()
        return total

    def spread_start(self, out, sems):
        mine = out.at[self.quarter(self.me)]
        far = self.copy(mine, mine, sems, 3, self.across)
        far.start()
        near = self.copy(mine, mine, sems, 4, self.beside)
        near.start()
        return (far, near)

    def spread_end(self, out, sems, copies):
        theirs = out.at[self.quarter(self.across)]
        self.copy(theirs, theirs, sems, 3, self.across).wait_recv()
        passed = self.copy(theirs, theirs, sems, 5, self.beside)
        passed.start()
        nearby = out.at[self.quarter(self.beside)]
        self.copy(nearby, nearby, sems, 4, self.beside).wait_recv()
        last = out.at[self.quarter(self.corner)]
        self.copy(last, last, sems, 5, self.beside).wait_recv()
        for copy in copies + (passed,):
            copy.wait_send()


def row_inverse(values):
    return lax.rsqrt(jnp.mean(values * values, axis=-1, keepdims=True) + EPS)


def second_norm_kernel(part, tokens, gain, hidden, second, held, sems):
    square = Square(part.shape[0])
    square.greet()
    copies = square.reduce_start(part, held, sems)
    copies = square.reduce_cross(part, held, sems, copies)
    total = square.reduce_end(part, held, copies)
    values = tokens[square.quarter(square.me), :].astype(jnp.float32) + total
    hidden[...] = values
    second[square.quarter(square.me), :] = (values * row_inverse(values) * gain[...]).astype(
        jnp.bfloat16
    )
    square.spread_end(second, sems, square.spread_start(second, sems))


def branch_kernel(
    d_second_part, ffn_part, hidden, cotangent, gain, d_hidden, d_branch, output, d_gain,
    held_a, held_b, sems_a, sems_b,
):
    square = Square(ffn_part.shape[0])
    mine = square.quarter(square.me)
    square.greet()
    copies_a = square.reduce_start(d_second_part, held_a, sems_a)
    copies_b = square.reduce_start(ffn_part, held_b, sems_b)
    copies_a = square.reduce_cross(d_second_part, held_a, sems_a, copies_a)
    copies_b = square.reduce_cross(ffn_part, held_b, sems_b, copies_b)
    d_second = square.reduce_end(d_second_part, held_a, copies_a)
    values = hidden[...]
    inverse = row_inverse(values)
    scaled = d_second * gain[...]
    d_values = inverse * scaled - values * inverse * inverse * inverse * jnp.mean(
        scaled * values, axis=-1, keepdims=True
    )
    d_total = cotangent[mine, :].astype(jnp.float32) + d_values
    d_hidden[...] = d_total
    d_branch[mine, :] = d_total.astype(jnp.bfloat16)
    spread_a = square.spread_start(d_branch, sems_a)
    d_gain[...] = jnp.sum(d_second * values * inverse, axis=0, keepdims=True)
    ffn = square.reduce_end(ffn_part, held_b, copies_b)
    output[mine, :] = (hidden[...] + ffn).astype(jnp.bfloat16)
    spread_b = square.spread_start(output, sems_b)
    square.spread_end(d_branch, sems_a, spread_a)
    square.spread_end(output, sems_b, spread_b)


def first_norm_kernel(
    part, tokens, gain, d_hidden, gains_in, d_tokens, gains_out, held, sems, slots, slot_sems
):
    square = Square(part.shape[0])
    mine = square.quarter(square.me)
    square.greet(everyone=True)
    copies = square.reduce_start(part, held, sems)
    copies = square.reduce_cross(part, held, sems, copies)
    d_first = square.reduce_end(part, held, copies)
    values = tokens[mine, :].astype(jnp.float32)
    inverse = row_inverse(values)
    scaled = d_first * gain[...]
    d_values = inverse * scaled - values * inverse * inverse * inverse * jnp.mean(
        scaled * values, axis=-1, keepdims=True
    )
    d_tokens[mine, :] = (d_hidden[...] + d_values).astype(jnp.bfloat16)
    spread = square.spread_start(d_tokens, sems)
    d_gain = jnp.sum(d_first * values * inverse, axis=0, keepdims=True)
    slots[square.me] = jnp.concatenate([d_gain, gains_in[0:7, :]], axis=0)
    own = slots.at[square.me]
    sent = []
    for index, other in enumerate((square.beside, square.across, square.corner)):
        sent.append(square.copy(own, own, slot_sems, index, other))
        sent[-1].start()
    square.spread_end(d_tokens, sems, spread)
    for index, other in enumerate((square.beside, square.across, square.corner)):
        theirs = slots.at[other]
        square.copy(theirs, theirs, slot_sems, index, other).wait_recv()
    for copy in sent:
        copy.wait_send()
    gains_out[...] = slots[0] + slots[1] + slots[2] + slots[3]


def square_call(kernel, ident, outs, held, extra, *operands):
    rows, width = operands[0].shape
    scratch = [pltpu.VMEM((4, rows // 4, width), jnp.bfloat16)] * held
    scratch += [pltpu.SemaphoreType.DMA((2, 6))] * held
    return pl.pallas_call(
        kernel,
        out_shape=[jax.ShapeDtypeStruct(shape, dtype) for shape, dtype in outs],
        in_specs=[whole_vmem()] * len(operands),
        out_specs=[whole_vmem()] * len(outs),
        scratch_shapes=scratch + extra,
        compiler_params=pltpu.CompilerParams(
            collective_id=ident, has_side_effects=True, vmem_limit_bytes=VMEM_BYTES
        ),
    )(*operands)


def padded_column(values, rows):
    return jnp.pad(values.reshape(-1, 1), ((0, rows - values.shape[0]), (0, 0)))


def per_device(
    n_dp,
    tokens,
    segment_ids,
    cotangent,
    attn_gain,
    query_gain,
    key_gain,
    w_query,
    w_key,
    w_value,
    w_out,
    ffn_gain,
    w_gate,
    w_up,
    w_down,
):
    rows = w_query.shape[0]
    count, width = tokens.shape
    gains = jnp.concatenate(
        [padded_column(item, rows) for item in (attn_gain, ffn_gain, query_gain, key_gain)], axis=1
    )
    gains = jnp.pad(gains, ((0, 0), (0, LANES - gains.shape[1])))
    packed_small = jnp.concatenate([w_query, w_key, w_value, w_out.T, gains], axis=1)
    packed_large = jnp.concatenate([w_gate, w_up, w_down.T], axis=1)
    small = ring_gather(packed_small, n_dp, 0)
    large = ring_gather(packed_large, n_dp, 1)
    q_width, k_width, o_width = (w_query.shape[1], w_key.shape[1], w_out.shape[0])
    f_width = w_gate.shape[1]
    edge_k = q_width + k_width
    edge_v = edge_k + k_width
    edge_o = edge_v + o_width
    project_full = small[:, :edge_v]
    out_full = small[:, edge_v:edge_o]
    columns = small[:, edge_o : edge_o + 4].astype(jnp.float32)
    gain_one = columns[:, 0]
    gain_two = columns[:, 1]
    small_gains = columns.reshape(n_dp, rows, 4)[:, : query_gain.shape[0], 2:]
    gain_query = small_gains[:, :, 0].reshape(-1)
    gain_key = small_gains[:, :, 1].reshape(-1)
    pair_full = large[:, : 2 * f_width]
    down_full = large[:, 2 * f_width :]

    head_dim = gain_query.shape[0]
    heads = q_width // head_dim
    kv_heads = k_width // head_dim
    group = heads // kv_heads
    span = min(512, count)
    blocks = count // span
    inputs = tokens.astype(jnp.float32)
    segs = segment_ids[0]
    cosine, sine = rotary_tables(positions(segs), head_dim)
    normed_one, _ = norm_forward(inputs, gain_one)
    first_in = normed_one.astype(jnp.bfloat16)
    projected = jnp.dot(first_in, project_full, preferred_element_type=jnp.float32)
    query_raw = projected[:, :q_width].reshape(count, heads, head_dim)
    key_raw = projected[:, q_width:edge_k].reshape(count, kv_heads, head_dim)
    value_low = projected[:, edge_k:].astype(jnp.bfloat16).reshape(count, kv_heads, head_dim)
    query_normed, query_inv = norm_forward(query_raw, gain_query)
    key_normed, key_inv = norm_forward(key_raw, gain_key)
    query_low = (
        rotate(query_normed, cosine, sine)
        .astype(jnp.bfloat16)
        .reshape(count, kv_heads, group, head_dim)
    )
    key_low = rotate(key_normed, cosine, sine).astype(jnp.bfloat16)
    key_pad = jnp.concatenate([jnp.zeros((span, kv_heads, head_dim), jnp.bfloat16), key_low])
    value_pad = jnp.concatenate([jnp.zeros((span, kv_heads, head_dim), jnp.bfloat16), value_low])
    seg_pad = jnp.concatenate([jnp.full((span,), -1, jnp.int32), segs])
    pieces = []
    totals = []
    for block in range(blocks):
        scores, _, keys = block_scores(query_low, key_pad, seg_pad, segs, block, span)
        peak = jnp.max(scores, axis=-1, keepdims=True)
        total = jnp.log(jnp.sum(jnp.exp(scores - peak), axis=-1, keepdims=True)) + peak
        probs = jnp.exp(scores - total).astype(jnp.bfloat16)
        values = value_pad[block * span : block * span + 2 * span]
        pieces.append(
            jnp.einsum("kgqj,jkd->qkgd", probs, values, preferred_element_type=jnp.float32)
        )
        totals.append(total)
    attended = jnp.concatenate(pieces).reshape(count, heads * head_dim).astype(jnp.bfloat16)
    attn_part = contract_cols(attended, out_full).astype(jnp.bfloat16)
    gain_row = gain_two.reshape(1, width)
    hidden, second_in = square_call(
        second_norm_kernel,
        4,
        [((count // 4, width), jnp.float32), ((count, width), jnp.bfloat16)],
        1,
        [],
        attn_part,
        tokens,
        gain_row,
    )
    pair = jnp.dot(second_in, pair_full, preferred_element_type=jnp.float32)
    gate_val = pair[:, :f_width]
    up_val = pair[:, f_width:]
    sigma = jax.nn.sigmoid(gate_val)
    activated = gate_val * sigma
    inner = (activated * up_val).astype(jnp.bfloat16)
    ffn_part = contract_cols(inner, down_full).astype(jnp.bfloat16)
    d_inner = jnp.dot(cotangent, down_full, preferred_element_type=jnp.float32)
    slope = sigma * (1.0 + gate_val * (1.0 - sigma))
    d_gate_low = (d_inner * up_val * slope).astype(jnp.bfloat16)
    d_up_low = (d_inner * activated).astype(jnp.bfloat16)
    d_pair_low = jnp.concatenate([d_gate_low, d_up_low], axis=1)
    d_second_part = contract_cols(d_pair_low, pair_full).astype(jnp.bfloat16)
    grad_large = jnp.concatenate(
        [
            contract_rows(second_in, d_pair_low).astype(jnp.bfloat16),
            contract_rows(cotangent, inner).astype(jnp.bfloat16),
        ],
        axis=1,
    )
    d_hidden, d_branch_low, output, d_gain_two = square_call(
        branch_kernel,
        5,
        [
            ((count // 4, width), jnp.float32),
            ((count, width), jnp.bfloat16),
            ((count, width), jnp.bfloat16),
            ((1, width), jnp.float32),
        ],
        2,
        [],
        d_second_part,
        ffn_part,
        hidden,
        cotangent,
        gain_row,
    )
    summed_large = ring_scatter(grad_large, n_dp, 2)
    d_out = contract_rows(d_branch_low, attended)
    d_attended = (
        jnp.dot(d_branch_low, out_full, preferred_element_type=jnp.float32)
        .astype(jnp.bfloat16)
        .reshape(count, kv_heads, group, head_dim)
    )
    d_query_parts = []
    d_key_pad = jnp.zeros((count + span, kv_heads, head_dim), jnp.float32)
    d_value_pad = jnp.zeros((count + span, kv_heads, head_dim), jnp.float32)
    for block in range(blocks):
        scores, queries, keys = block_scores(query_low, key_pad, seg_pad, segs, block, span)
        probs = jnp.exp(scores - totals[block])
        values = value_pad[block * span : block * span + 2 * span]
        d_rows = d_attended[block * span : (block + 1) * span]
        d_probs = jnp.einsum("qkgd,jkd->kgqj", d_rows, values, preferred_element_type=jnp.float32)
        inner_sum = jnp.sum(probs * d_probs, axis=-1, keepdims=True)
        d_scores = (probs * (d_probs - inner_sum)).astype(jnp.bfloat16)
        d_query_parts.append(
            jnp.einsum("kgqj,jkd->qkgd", d_scores, keys, preferred_element_type=jnp.float32) * SCALE
        )
        key_term = (
            jnp.einsum("kgqj,qkgd->jkd", d_scores, queries, preferred_element_type=jnp.float32)
            * SCALE
        )
        value_term = jnp.einsum(
            "kgqj,qkgd->jkd", probs.astype(jnp.bfloat16), d_rows, preferred_element_type=jnp.float32
        )
        d_key_pad = d_key_pad.at[block * span : block * span + 2 * span].add(key_term)
        d_value_pad = d_value_pad.at[block * span : block * span + 2 * span].add(value_term)
    d_query_rot = jnp.concatenate(d_query_parts).reshape(count, heads, head_dim)
    d_query_raw, d_gain_query = norm_backward(
        unrotate(d_query_rot, cosine, sine), query_raw, query_inv, gain_query
    )
    d_key_raw, d_gain_key = norm_backward(
        unrotate(d_key_pad[span:], cosine, sine), key_raw, key_inv, gain_key
    )
    d_projected = jnp.concatenate(
        [
            d_query_raw.reshape(count, heads * head_dim).astype(jnp.bfloat16),
            d_key_raw.reshape(count, kv_heads * head_dim).astype(jnp.bfloat16),
            d_value_pad[span:].reshape(count, kv_heads * head_dim).astype(jnp.bfloat16),
        ],
        axis=1,
    )
    d_project = contract_rows(first_in, d_projected)
    d_first_part = contract_cols(d_projected, project_full).astype(jnp.bfloat16)
    head_gains = jnp.concatenate([d_gain_query, d_gain_key])
    head_gains = jnp.pad(head_gains, (0, width - 2 * head_dim)).reshape(1, width)
    d_tokens_low, d_gains = square_call(
        first_norm_kernel,
        6,
        [((count, width), jnp.bfloat16), ((8, width), jnp.float32)],
        1,
        [pltpu.VMEM((4, 8, width), jnp.float32), pltpu.SemaphoreType.DMA((2, 3))],
        d_first_part,
        tokens,
        gain_one.reshape(1, width),
        d_hidden,
        jnp.concatenate([d_gain_two, head_gains, jnp.zeros((6, width), jnp.float32)]),
    )
    per_head = d_gains[2, : 2 * head_dim].reshape(2, n_dp, head_dim // n_dp)
    per_head = jnp.pad(per_head, ((0, 0), (0, 0), (0, rows - head_dim // n_dp)))
    gain_columns = jnp.stack(
        [d_gains[0], d_gains[1], per_head[0].reshape(-1), per_head[1].reshape(-1)], axis=1
    )
    gain_columns = jnp.pad(gain_columns, ((0, 0), (0, LANES - 4)))
    grad_small = jnp.concatenate(
        [
            d_project.astype(jnp.bfloat16),
            d_out.astype(jnp.bfloat16),
            gain_columns.astype(jnp.bfloat16),
        ],
        axis=1,
    )
    summed_small = ring_scatter(grad_small, n_dp, 3)
    return (
        output,
        d_tokens_low.astype(jnp.float32),
        summed_small[:, edge_o],
        summed_small[: head_dim // n_dp, edge_o + 2],
        summed_small[: head_dim // n_dp, edge_o + 3],
        summed_small[:, :q_width],
        summed_small[:, q_width:edge_k],
        summed_small[:, edge_k:edge_v],
        summed_small[:, edge_v:edge_o].T,
        summed_small[:, edge_o + 1],
        summed_large[:, :f_width],
        summed_large[:, f_width : 2 * f_width],
        summed_large[:, 2 * f_width :].T,
    )


def solution(mesh):
    in_specs = (
        P("dp", None),
        P("dp", None),
        P("dp", None),
        P("dp"),
        P("dp"),
        P("dp"),
        P("dp", "tensor"),
        P("dp", "tensor"),
        P("dp", "tensor"),
        P("tensor", "dp"),
        P("dp"),
        P("dp", "tensor"),
        P("dp", "tensor"),
        P("tensor", "dp"),
    )
    out_specs = (
        P("dp", None),
        P("dp", None),
        P("dp"),
        P("dp"),
        P("dp"),
        P("dp", "tensor"),
        P("dp", "tensor"),
        P("dp", "tensor"),
        P("tensor", "dp"),
        P("dp"),
        P("dp", "tensor"),
        P("dp", "tensor"),
        P("tensor", "dp"),
    )
    body = functools.partial(per_device, mesh.shape["dp"])
    return jax.shard_map(
        body, mesh=mesh, in_specs=in_specs, out_specs=out_specs, check_vma=False
    )
```

```python
import functools

import jax
import jax.numpy as jnp
from jax import lax
from jax.experimental import pallas as pl
from jax.experimental.pallas import tpu as pltpu
from jax.sharding import PartitionSpec as P

EPS = 1e-05
THETA = 1000000.0
SCALE = 0.125


def positions(segs):
    count = segs.shape[0]
    index = jnp.arange(count, dtype=jnp.int32)
    starts = jnp.concatenate([jnp.ones((1,), dtype=bool), segs[1:] != segs[:-1]])
    first = lax.cummax(jnp.where(starts, index, jnp.zeros_like(index)), axis=0)
    return index - first


def rotary_tables(pos, width):
    half = width // 2
    freq = THETA ** (-(jnp.arange(half, dtype=jnp.float32) * 2.0) / width)
    angle = pos.astype(jnp.float32)[:, None] * freq[None, :]
    return (jnp.cos(angle), jnp.sin(angle))


def rotate(values, cosine, sine):
    half = values.shape[-1] // 2
    first, second = (values[..., :half], values[..., half:])
    cos_b = cosine[:, None, :]
    sin_b = sine[:, None, :]
    return jnp.concatenate(
        [first * cos_b - second * sin_b, second * cos_b + first * sin_b], axis=-1
    )


def unrotate(grads, cosine, sine):
    half = grads.shape[-1] // 2
    first, second = (grads[..., :half], grads[..., half:])
    cos_b = cosine[:, None, :]
    sin_b = sine[:, None, :]
    return jnp.concatenate(
        [first * cos_b + second * sin_b, second * cos_b - first * sin_b], axis=-1
    )


def norm_forward(values, gain):
    inverse = lax.rsqrt(jnp.mean(values * values, axis=-1, keepdims=True) + EPS)
    return (values * inverse * gain, inverse)


def norm_backward(grad_normed, values, inverse, gain):
    scaled = grad_normed * gain
    d_values = inverse * scaled - values * inverse * inverse * inverse * jnp.mean(
        scaled * values, axis=-1, keepdims=True
    )
    flat = (grad_normed * values * inverse).reshape(-1, values.shape[-1])
    return (d_values, jnp.sum(flat, axis=0))


def contract_rows(left, right):
    return lax.dot_general(
        left, right, (((0,), (0,)), ((), ())), preferred_element_type=jnp.float32
    )


def contract_cols(left, right):
    return lax.dot_general(
        left, right, (((1,), (1,)), ((), ())), preferred_element_type=jnp.float32
    )


def block_scores(query_low, key_pad, seg_pad, segs, block, span):
    rows = query_low[block * span : (block + 1) * span]
    keys = key_pad[block * span : block * span + 2 * span]
    scores = jnp.einsum("qkgd,jkd->kgqj", rows, keys, preferred_element_type=jnp.float32) * SCALE
    row_index = block * span + jnp.arange(span, dtype=jnp.int32)
    key_index = block * span - span + jnp.arange(2 * span, dtype=jnp.int32)
    same = (
        seg_pad[block * span : block * span + 2 * span][None, :]
        == segs[block * span : (block + 1) * span][:, None]
    )
    allowed = same & (key_index[None, :] <= row_index[:, None])
    return (jnp.where(allowed, scores, -1e30), rows, keys)


MESH = pl.DeviceIdType.MESH
ANYWHERE = pl.BlockSpec(memory_space=pl.ANY)
VMEM_BYTES = 48 * 1024 * 1024
LANES = 128


def whole_vmem():
    return pl.BlockSpec(memory_space=pltpu.VMEM)


def ring_place(index, count):
    odd = lax.rem(index, 2)
    half = lax.div(index, 2)
    return (1 - odd) * half + odd * (count - 1 - half)


def ring_index(place, count):
    second = lax.div(place, count // 2)
    return (1 - second) * 2 * place + second * (2 * (count - 1 - place) + 1)


def ring_parts(width):
    tiles = width // LANES
    cuts = [0, (tiles + 3) // 4, (tiles + 1) // 2, (3 * tiles + 3) // 4, tiles]
    return [
        (cuts[i] * LANES, (cuts[i + 1] - cuts[i]) * LANES, 1 if i < 2 else -1) for i in (0, 2, 1, 3)
    ]


def greet(neighbours):
    barrier = pltpu.get_barrier_semaphore()
    for axis, neighbour in neighbours:
        pl.semaphore_signal(barrier, inc=1, device_id={axis: neighbour}, device_id_type=MESH)
    pl.semaphore_wait(barrier, len(neighbours))


def ring_neighbours(count):
    me = ring_place(lax.axis_index("dp"), count)
    return [("dp", ring_index(lax.rem(me + way + count, count), count)) for way in (1, -1)]


def gather_steps(count, x_ref, o_ref, own_sem, send_sem, recv_sem, met=False):
    me = ring_place(lax.axis_index("dp"), count)
    rows = x_ref.shape[0]
    parts = ring_parts(x_ref.shape[1])
    towards = {way: ring_index(lax.rem(me + way + count, count), count) for way in (1, -1)}
    if not met:
        greet([("dp", towards[1]), ("dp", towards[-1])])

    def block(place, part):
        start, width, _ = parts[part]
        first = pl.multiple_of(ring_index(lax.rem(place + 2 * count, count), count) * rows, rows)
        return o_ref.at[pl.ds(first, rows), pl.ds(start, width)]

    def copy(step, part, source, place):
        start, width, way = parts[part]
        return pltpu.make_async_remote_copy(
            src_ref=source,
            dst_ref=block(place, part),
            send_sem=send_sem.at[part, step],
            recv_sem=recv_sem.at[part, step],
            device_id={"dp": towards[way]},
            device_id_type=MESH,
        )

    def outgoing(step, part):
        place = me - parts[part][2] * step
        return copy(step, part, block(place, part), place)

    def incoming(step, part):
        place = me - parts[part][2] * (step + 1)
        return copy(step, part, block(place, part), place)

    for part, (start, width, _) in enumerate(parts):
        copy(0, part, x_ref.at[:, pl.ds(start, width)], me).start()
    first = pl.multiple_of(ring_index(me, count) * rows, rows)
    own = pltpu.make_async_copy(x_ref, o_ref.at[pl.ds(first, rows)], own_sem)
    own.start()

    for step in range(1, count - 1):
        yield
        for part in range(len(parts)):
            incoming(step - 1, part).wait_recv()
            outgoing(step, part).start()
    yield

    def settle(step, carry):
        for part in range(len(parts)):
            outgoing(step, part).wait_send()
        return carry

    for part in range(len(parts)):
        incoming(count - 2, part).wait_recv()
    lax.fori_loop(0, count - 1, settle, 0)
    own.wait()


def run_all(steps):
    for _ in steps:
        pass


def run_turns(*all_steps):
    waiting = list(all_steps)
    while waiting:
        waiting = [steps for steps in waiting if next(steps, waiting) is not waiting]


def gather_kernel(*refs):
    run_all(gather_steps(*refs))


def scatter_kernel(*refs):
    run_all(scatter_steps(*refs))


def ring_gather(shard, count, ident):
    rows, width = shard.shape
    return pl.pallas_call(
        functools.partial(gather_kernel, count),
        out_shape=jax.ShapeDtypeStruct((rows * count, width), shard.dtype),
        in_specs=[pl.BlockSpec(memory_space=pl.ANY)],
        out_specs=pl.BlockSpec(memory_space=pl.ANY),
        scratch_shapes=[
            pltpu.SemaphoreType.DMA,
            pltpu.SemaphoreType.DMA((4, count - 1)),
            pltpu.SemaphoreType.DMA((4, count - 1)),
        ],
        compiler_params=pltpu.CompilerParams(
            collective_id=ident, has_side_effects=True, vmem_limit_bytes=VMEM_BYTES
        ),
    )(shard)


def scatter_steps(count, g_ref, o_ref, held, send_sem, recv_sem, met=False):
    me = ring_place(lax.axis_index("dp"), count)
    rows = o_ref.shape[0]
    parts = ring_parts(o_ref.shape[1])
    towards = {way: ring_index(lax.rem(me + way + count, count), count) for way in (1, -1)}
    if not met:
        greet([("dp", towards[1]), ("dp", towards[-1])])

    def term(place, part):
        start, width, _ = parts[part]
        first = pl.multiple_of(ring_index(lax.rem(place + 2 * count, count), count) * rows, rows)
        return g_ref.at[pl.ds(first, rows), pl.ds(start, width)]

    def slot(step, part):
        start, width, _ = parts[part]
        return held.at[step, :, pl.ds(start, width)]

    def copy(step, part, source):
        return pltpu.make_async_remote_copy(
            src_ref=source,
            dst_ref=slot(step, part),
            send_sem=send_sem.at[part, step],
            recv_sem=recv_sem.at[part, step],
            device_id={"dp": towards[parts[part][2]]},
            device_id_type=MESH,
        )

    for part, (_, _, way) in enumerate(parts):
        copy(0, part, term(me - way, part)).start()

    for step in range(1, count - 1):
        yield
        for part, (_, _, way) in enumerate(parts):
            copy(step - 1, part, slot(step - 1, part)).wait_recv()
            mine = term(me - way * (step + 1), part)
            both = slot(step - 1, part)
            both[...] = (both[...].astype(jnp.float32) + mine[...].astype(jnp.float32)).astype(
                jnp.bfloat16
            )
            copy(step, part, both).start()
    yield
    for part, (start, width, _) in enumerate(parts):
        copy(count - 2, part, slot(count - 2, part)).wait_recv()
        o_ref[:, pl.ds(start, width)] = slot(count - 2, part)[...].astype(jnp.float32) + term(
            me, part
        )[...].astype(jnp.float32)

    def settle(step, carry):
        for part in range(len(parts)):
            copy(step, part, slot(step, part)).wait_send()
        return carry

    lax.fori_loop(0, count - 1, settle, 0)


def ring_scatter(terms, count, ident):
    total, width = terms.shape
    rows = total // count
    return pl.pallas_call(
        functools.partial(scatter_kernel, count),
        out_shape=jax.ShapeDtypeStruct((rows, width), jnp.float32),
        in_specs=[whole_vmem()],
        out_specs=whole_vmem(),
        scratch_shapes=[
            pltpu.VMEM((count - 1, rows, width), jnp.bfloat16),
            pltpu.SemaphoreType.DMA((4, count - 1)),
            pltpu.SemaphoreType.DMA((4, count - 1)),
        ],
        compiler_params=pltpu.CompilerParams(
            collective_id=ident, has_side_effects=True, vmem_limit_bytes=VMEM_BYTES
        ),
    )(terms)


class Square:
    def __init__(self, rows):
        self.me = lax.axis_index("tensor")
        self.core = lax.rem(self.me, 2)
        self.chip = lax.div(self.me, 2)
        self.beside = self.me + 1 - 2 * self.core
        self.across = lax.rem(self.me + 2, 4)
        self.corner = lax.rem(self.beside + 2, 4)
        self.rows = rows // 4

    def quarter(self, index):
        return pl.ds(pl.multiple_of(index * self.rows, self.rows), self.rows)

    def neighbours(self, everyone=False):
        partners = [("tensor", self.beside), ("tensor", self.across)]
        return partners + ([("tensor", self.corner)] if everyone else [])

    def copy(self, source, target, sems, index, other):
        return pltpu.make_async_remote_copy(
            src_ref=source,
            dst_ref=target,
            send_sem=sems.at[0, index],
            recv_sem=sems.at[1, index],
            device_id={"tensor": other},
            device_id_type=MESH,
        )

    def reduce_start(self, part, held, sems):
        first = self.copy(
            part.at[self.quarter(self.corner)], held.at[0], sems, 0, self.beside
        )
        first.start()
        second = self.copy(
            part.at[self.quarter(self.beside)], held.at[1], sems, 1, self.beside
        )
        second.start()
        return (first, second)

    def reduce_cross(self, part, held, sems, copies):
        copies[0].wait_recv()
        held[3] = (
            part[self.quarter(self.across), :].astype(jnp.float32) + held[0].astype(jnp.float32)
        ).astype(jnp.bfloat16)
        third = self.copy(held.at[3], held.at[2], sems, 2, self.across)
        third.start()
        return copies + (third,)

    def reduce_end(self, part, held, copies):
        copies[1].wait_recv()
        near = part[self.quarter(self.me), :].astype(jnp.float32) + held[1].astype(jnp.float32)
        copies[2].wait_recv()
        total = near + held[2].astype(jnp.float32)
        for copy in copies:
            copy.wait_send()
        return total

    def spread_start(self, out, sems):
        mine = out.at[self.quarter(self.me)]
        far = self.copy(mine, mine, sems, 3, self.across)
        far.start()
        near = self.copy(mine, mine, sems, 4, self.beside)
        near.start()
        return (far, near)

    def spread_end(self, out, sems, copies):
        self.spread_close(out, sems, self.spread_pass(out, sems, copies))

    def spread_pass(self, out, sems, copies):
        theirs = out.at[self.quarter(self.across)]
        self.copy(theirs, theirs, sems, 3, self.across).wait_recv()
        passed = self.copy(theirs, theirs, sems, 5, self.beside)
        passed.start()
        return copies + (passed,)

    def spread_close(self, out, sems, copies):
        nearby = out.at[self.quarter(self.beside)]
        self.copy(nearby, nearby, sems, 4, self.beside).wait_recv()
        last = out.at[self.quarter(self.corner)]
        self.copy(last, last, sems, 5, self.beside).wait_recv()
        for copy in copies:
            copy.wait_send()


def row_inverse(values):
    return lax.rsqrt(jnp.mean(values * values, axis=-1, keepdims=True) + EPS)


def second_norm_steps(square, part, tokens, gain, hidden, second, held, sems):
    copies = square.reduce_start(part, held, sems)
    yield
    copies = square.reduce_cross(part, held, sems, copies)
    yield
    total = square.reduce_end(part, held, copies)
    values = tokens[square.quarter(square.me), :].astype(jnp.float32) + total
    hidden[...] = values
    second[square.quarter(square.me), :] = (values * row_inverse(values) * gain[...]).astype(
        jnp.bfloat16
    )
    spread = square.spread_start(second, sems)
    yield
    yield
    spread = square.spread_pass(second, sems, spread)
    yield
    square.spread_close(second, sems, spread)


def second_norm_kernel(
    count, part, tokens, gain, shard, hidden, second, full, held, sems, own_sem, send_sem, recv_sem
):
    square = Square(part.shape[0])
    greet(square.neighbours() + ring_neighbours(count))
    run_turns(
        second_norm_steps(square, part, tokens, gain, hidden, second, held, sems),
        gather_steps(count, shard, full, own_sem, send_sem, recv_sem, met=True),
    )


def branch_steps(
    square, d_second_part, ffn_part, hidden, cotangent, gain, d_hidden, d_branch, output, d_gain,
    held_a, held_b, sems_a, sems_b,
):
    mine = square.quarter(square.me)
    copies_a = square.reduce_start(d_second_part, held_a, sems_a)
    copies_b = square.reduce_start(ffn_part, held_b, sems_b)
    yield
    copies_a = square.reduce_cross(d_second_part, held_a, sems_a, copies_a)
    copies_b = square.reduce_cross(ffn_part, held_b, sems_b, copies_b)
    yield
    d_second = square.reduce_end(d_second_part, held_a, copies_a)
    values = hidden[...]
    inverse = row_inverse(values)
    scaled = d_second * gain[...]
    d_values = inverse * scaled - values * inverse * inverse * inverse * jnp.mean(
        scaled * values, axis=-1, keepdims=True
    )
    d_total = cotangent[mine, :].astype(jnp.float32) + d_values
    d_hidden[...] = d_total
    d_branch[mine, :] = d_total.astype(jnp.bfloat16)
    spread_a = square.spread_start(d_branch, sems_a)
    d_gain[...] = jnp.sum(d_second * values * inverse, axis=0, keepdims=True)
    yield
    ffn = square.reduce_end(ffn_part, held_b, copies_b)
    output[mine, :] = (hidden[...] + ffn).astype(jnp.bfloat16)
    spread_b = square.spread_start(output, sems_b)
    yield
    spread_a = square.spread_pass(d_branch, sems_a, spread_a)
    yield
    spread_b = square.spread_pass(output, sems_b, spread_b)
    yield
    square.spread_close(d_branch, sems_a, spread_a)
    square.spread_close(output, sems_b, spread_b)


def branch_kernel(
    count, d_second_part, ffn_part, hidden, cotangent, gain, terms,
    d_hidden, d_branch, output, d_gain, summed,
    held_a, held_b, sems_a, sems_b, moving, send_sem, recv_sem,
):
    square = Square(ffn_part.shape[0])
    greet(square.neighbours() + ring_neighbours(count))
    run_turns(
        branch_steps(
            square, d_second_part, ffn_part, hidden, cotangent, gain, d_hidden, d_branch, output,
            d_gain, held_a, held_b, sems_a, sems_b,
        ),
        scatter_steps(count, terms, summed, moving, send_sem, recv_sem, met=True),
    )


def first_norm_kernel(
    part, tokens, gain, d_hidden, gains_in, d_tokens, gains_out, held, sems, slots, slot_sems
):
    square = Square(part.shape[0])
    mine = square.quarter(square.me)
    greet(square.neighbours(everyone=True))
    copies = square.reduce_start(part, held, sems)
    copies = square.reduce_cross(part, held, sems, copies)
    d_first = square.reduce_end(part, held, copies)
    values = tokens[mine, :].astype(jnp.float32)
    inverse = row_inverse(values)
    scaled = d_first * gain[...]
    d_values = inverse * scaled - values * inverse * inverse * inverse * jnp.mean(
        scaled * values, axis=-1, keepdims=True
    )
    d_tokens[mine, :] = (d_hidden[...] + d_values).astype(jnp.bfloat16)
    spread = square.spread_start(d_tokens, sems)
    d_gain = jnp.sum(d_first * values * inverse, axis=0, keepdims=True)
    slots[square.me] = jnp.concatenate([d_gain, gains_in[0:7, :]], axis=0)
    own = slots.at[square.me]
    sent = []
    for index, other in enumerate((square.beside, square.across, square.corner)):
        sent.append(square.copy(own, own, slot_sems, index, other))
        sent[-1].start()
    square.spread_end(d_tokens, sems, spread)
    for index, other in enumerate((square.beside, square.across, square.corner)):
        theirs = slots.at[other]
        square.copy(theirs, theirs, slot_sems, index, other).wait_recv()
    for copy in sent:
        copy.wait_send()
    gains_out[...] = slots[0] + slots[1] + slots[2] + slots[3]


def square_call(kernel, ident, outs, held, extra, *operands, hbm_in=(), hbm_out=()):
    rows, width = operands[0].shape
    scratch = [pltpu.VMEM((4, rows // 4, width), jnp.bfloat16)] * held
    scratch += [pltpu.SemaphoreType.DMA((2, 6))] * held
    return pl.pallas_call(
        kernel,
        out_shape=[jax.ShapeDtypeStruct(shape, dtype) for shape, dtype in outs],
        in_specs=[ANYWHERE if at in hbm_in else whole_vmem() for at in range(len(operands))],
        out_specs=[ANYWHERE if at in hbm_out else whole_vmem() for at in range(len(outs))],
        scratch_shapes=scratch + extra,
        compiler_params=pltpu.CompilerParams(
            collective_id=ident, has_side_effects=True, vmem_limit_bytes=VMEM_BYTES
        ),
    )(*operands)


def padded_column(values, rows):
    return jnp.pad(values.reshape(-1, 1), ((0, rows - values.shape[0]), (0, 0)))


def per_device(
    n_dp,
    tokens,
    segment_ids,
    cotangent,
    attn_gain,
    query_gain,
    key_gain,
    w_query,
    w_key,
    w_value,
    w_out,
    ffn_gain,
    w_gate,
    w_up,
    w_down,
):
    rows = w_query.shape[0]
    count, width = tokens.shape
    gains = jnp.concatenate(
        [padded_column(item, rows) for item in (attn_gain, ffn_gain, query_gain, key_gain)], axis=1
    )
    gains = jnp.pad(gains, ((0, 0), (0, LANES - gains.shape[1])))
    packed_small = jnp.concatenate([w_query, w_key, w_value, w_out.T, gains], axis=1)
    packed_large = jnp.concatenate([w_gate, w_up, w_down.T], axis=1)
    small = ring_gather(packed_small, n_dp, 0)
    q_width, k_width, o_width = (w_query.shape[1], w_key.shape[1], w_out.shape[0])
    f_width = w_gate.shape[1]
    edge_k = q_width + k_width
    edge_v = edge_k + k_width
    edge_o = edge_v + o_width
    project_full = small[:, :edge_v]
    out_full = small[:, edge_v:edge_o]
    columns = small[:, edge_o : edge_o + 4].astype(jnp.float32)
    gain_one = columns[:, 0]
    gain_two = columns[:, 1]
    small_gains = columns.reshape(n_dp, rows, 4)[:, : query_gain.shape[0], 2:]
    gain_query = small_gains[:, :, 0].reshape(-1)
    gain_key = small_gains[:, :, 1].reshape(-1)

    head_dim = gain_query.shape[0]
    heads = q_width // head_dim
    kv_heads = k_width // head_dim
    group = heads // kv_heads
    span = min(512, count)
    blocks = count // span
    inputs = tokens.astype(jnp.float32)
    segs = segment_ids[0]
    cosine, sine = rotary_tables(positions(segs), head_dim)
    normed_one, _ = norm_forward(inputs, gain_one)
    first_in = normed_one.astype(jnp.bfloat16)
    projected = jnp.dot(first_in, project_full, preferred_element_type=jnp.float32)
    query_raw = projected[:, :q_width].reshape(count, heads, head_dim)
    key_raw = projected[:, q_width:edge_k].reshape(count, kv_heads, head_dim)
    value_low = projected[:, edge_k:].astype(jnp.bfloat16).reshape(count, kv_heads, head_dim)
    query_normed, query_inv = norm_forward(query_raw, gain_query)
    key_normed, key_inv = norm_forward(key_raw, gain_key)
    query_low = (
        rotate(query_normed, cosine, sine)
        .astype(jnp.bfloat16)
        .reshape(count, kv_heads, group, head_dim)
    )
    key_low = rotate(key_normed, cosine, sine).astype(jnp.bfloat16)
    key_pad = jnp.concatenate([jnp.zeros((span, kv_heads, head_dim), jnp.bfloat16), key_low])
    value_pad = jnp.concatenate([jnp.zeros((span, kv_heads, head_dim), jnp.bfloat16), value_low])
    seg_pad = jnp.concatenate([jnp.full((span,), -1, jnp.int32), segs])
    pieces = []
    totals = []
    for block in range(blocks):
        scores, _, keys = block_scores(query_low, key_pad, seg_pad, segs, block, span)
        peak = jnp.max(scores, axis=-1, keepdims=True)
        total = jnp.log(jnp.sum(jnp.exp(scores - peak), axis=-1, keepdims=True)) + peak
        probs = jnp.exp(scores - total).astype(jnp.bfloat16)
        values = value_pad[block * span : block * span + 2 * span]
        pieces.append(
            jnp.einsum("kgqj,jkd->qkgd", probs, values, preferred_element_type=jnp.float32)
        )
        totals.append(total)
    attended = jnp.concatenate(pieces).reshape(count, heads * head_dim).astype(jnp.bfloat16)
    attn_part = contract_cols(attended, out_full).astype(jnp.bfloat16)
    gain_row = gain_two.reshape(1, width)
    ring_sems = [pltpu.SemaphoreType.DMA((4, n_dp - 1))] * 2
    hidden, second_in, large = square_call(
        functools.partial(second_norm_kernel, n_dp),
        4,
        [
            ((count // 4, width), jnp.float32),
            ((count, width), jnp.bfloat16),
            ((n_dp * rows, packed_large.shape[1]), jnp.bfloat16),
        ],
        1,
        [pltpu.SemaphoreType.DMA] + ring_sems,
        attn_part,
        tokens,
        gain_row,
        packed_large,
        hbm_in=(3,),
        hbm_out=(2,),
    )
    pair_full = large[:, : 2 * f_width]
    down_full = large[:, 2 * f_width :]
    pair = jnp.dot(second_in, pair_full, preferred_element_type=jnp.float32)
    gate_val = pair[:, :f_width]
    up_val = pair[:, f_width:]
    sigma = jax.nn.sigmoid(gate_val)
    activated = gate_val * sigma
    inner = (activated * up_val).astype(jnp.bfloat16)
    ffn_part = contract_cols(inner, down_full).astype(jnp.bfloat16)
    d_inner = jnp.dot(cotangent, down_full, preferred_element_type=jnp.float32)
    slope = sigma * (1.0 + gate_val * (1.0 - sigma))
    d_gate_low = (d_inner * up_val * slope).astype(jnp.bfloat16)
    d_up_low = (d_inner * activated).astype(jnp.bfloat16)
    d_pair_low = jnp.concatenate([d_gate_low, d_up_low], axis=1)
    d_second_part = contract_cols(d_pair_low, pair_full).astype(jnp.bfloat16)
    grad_large = jnp.concatenate(
        [
            contract_rows(second_in, d_pair_low).astype(jnp.bfloat16),
            contract_rows(cotangent, inner).astype(jnp.bfloat16),
        ],
        axis=1,
    )
    d_hidden, d_branch_low, output, d_gain_two, summed_large = square_call(
        functools.partial(branch_kernel, n_dp),
        5,
        [
            ((count // 4, width), jnp.float32),
            ((count, width), jnp.bfloat16),
            ((count, width), jnp.bfloat16),
            ((1, width), jnp.float32),
            ((rows, grad_large.shape[1]), jnp.float32),
        ],
        2,
        [pltpu.VMEM((n_dp - 1, rows, grad_large.shape[1]), jnp.bfloat16)] + ring_sems,
        d_second_part,
        ffn_part,
        hidden,
        cotangent,
        gain_row,
        grad_large,
    )
    d_out = contract_rows(d_branch_low, attended)
    d_attended = (
        jnp.dot(d_branch_low, out_full, preferred_element_type=jnp.float32)
        .astype(jnp.bfloat16)
        .reshape(count, kv_heads, group, head_dim)
    )
    d_query_parts = []
    d_key_pad = jnp.zeros((count + span, kv_heads, head_dim), jnp.float32)
    d_value_pad = jnp.zeros((count + span, kv_heads, head_dim), jnp.float32)
    for block in range(blocks):
        scores, queries, keys = block_scores(query_low, key_pad, seg_pad, segs, block, span)
        probs = jnp.exp(scores - totals[block])
        values = value_pad[block * span : block * span + 2 * span]
        d_rows = d_attended[block * span : (block + 1) * span]
        d_probs = jnp.einsum("qkgd,jkd->kgqj", d_rows, values, preferred_element_type=jnp.float32)
        inner_sum = jnp.sum(probs * d_probs, axis=-1, keepdims=True)
        d_scores = (probs * (d_probs - inner_sum)).astype(jnp.bfloat16)
        d_query_parts.append(
            jnp.einsum("kgqj,jkd->qkgd", d_scores, keys, preferred_element_type=jnp.float32) * SCALE
        )
        key_term = (
            jnp.einsum("kgqj,qkgd->jkd", d_scores, queries, preferred_element_type=jnp.float32)
            * SCALE
        )
        value_term = jnp.einsum(
            "kgqj,qkgd->jkd", probs.astype(jnp.bfloat16), d_rows, preferred_element_type=jnp.float32
        )
        d_key_pad = d_key_pad.at[block * span : block * span + 2 * span].add(key_term)
        d_value_pad = d_value_pad.at[block * span : block * span + 2 * span].add(value_term)
    d_query_rot = jnp.concatenate(d_query_parts).reshape(count, heads, head_dim)
    d_query_raw, d_gain_query = norm_backward(
        unrotate(d_query_rot, cosine, sine), query_raw, query_inv, gain_query
    )
    d_key_raw, d_gain_key = norm_backward(
        unrotate(d_key_pad[span:], cosine, sine), key_raw, key_inv, gain_key
    )
    d_projected = jnp.concatenate(
        [
            d_query_raw.reshape(count, heads * head_dim).astype(jnp.bfloat16),
            d_key_raw.reshape(count, kv_heads * head_dim).astype(jnp.bfloat16),
            d_value_pad[span:].reshape(count, kv_heads * head_dim).astype(jnp.bfloat16),
        ],
        axis=1,
    )
    d_project = contract_rows(first_in, d_projected)
    d_first_part = contract_cols(d_projected, project_full).astype(jnp.bfloat16)
    head_gains = jnp.concatenate([d_gain_query, d_gain_key])
    head_gains = jnp.pad(head_gains, (0, width - 2 * head_dim)).reshape(1, width)
    d_tokens_low, d_gains = square_call(
        first_norm_kernel,
        6,
        [((count, width), jnp.bfloat16), ((8, width), jnp.float32)],
        1,
        [pltpu.VMEM((4, 8, width), jnp.float32), pltpu.SemaphoreType.DMA((2, 3))],
        d_first_part,
        tokens,
        gain_one.reshape(1, width),
        d_hidden,
        jnp.concatenate([d_gain_two, head_gains, jnp.zeros((6, width), jnp.float32)]),
    )
    per_head = d_gains[2, : 2 * head_dim].reshape(2, n_dp, head_dim // n_dp)
    per_head = jnp.pad(per_head, ((0, 0), (0, 0), (0, rows - head_dim // n_dp)))
    gain_columns = jnp.stack(
        [d_gains[0], d_gains[1], per_head[0].reshape(-1), per_head[1].reshape(-1)], axis=1
    )
    gain_columns = jnp.pad(gain_columns, ((0, 0), (0, LANES - 4)))
    grad_small = jnp.concatenate(
        [
            d_project.astype(jnp.bfloat16),
            d_out.astype(jnp.bfloat16),
            gain_columns.astype(jnp.bfloat16),
        ],
        axis=1,
    )
    summed_small = ring_scatter(grad_small, n_dp, 3)
    return (
        output,
        d_tokens_low.astype(jnp.float32),
        summed_small[:, edge_o],
        summed_small[: head_dim // n_dp, edge_o + 2],
        summed_small[: head_dim // n_dp, edge_o + 3],
        summed_small[:, :q_width],
        summed_small[:, q_width:edge_k],
        summed_small[:, edge_k:edge_v],
        summed_small[:, edge_v:edge_o].T,
        summed_small[:, edge_o + 1],
        summed_large[:, :f_width],
        summed_large[:, f_width : 2 * f_width],
        summed_large[:, 2 * f_width :].T,
    )


def solution(mesh):
    in_specs = (
        P("dp", None),
        P("dp", None),
        P("dp", None),
        P("dp"),
        P("dp"),
        P("dp"),
        P("dp", "tensor"),
        P("dp", "tensor"),
        P("dp", "tensor"),
        P("tensor", "dp"),
        P("dp"),
        P("dp", "tensor"),
        P("dp", "tensor"),
        P("tensor", "dp"),
    )
    out_specs = (
        P("dp", None),
        P("dp", None),
        P("dp"),
        P("dp"),
        P("dp"),
        P("dp", "tensor"),
        P("dp", "tensor"),
        P("dp", "tensor"),
        P("tensor", "dp"),
        P("dp"),
        P("dp", "tensor"),
        P("dp", "tensor"),
        P("tensor", "dp"),
    )
    body = functools.partial(per_device, mesh.shape["dp"])
    return jax.shard_map(
        body, mesh=mesh, in_specs=in_specs, out_specs=out_specs, check_vma=False
    )
```
